512 devices in a mesh: dp: 64 (over y_hi, x, z), mp: 8 (over y_lo, core).
Axes of the slice: x: 4, y: 8 (y_hi: 2, y_lo: 4; y = y_hi * 4 + y_lo), z: 8, core: 2. Of those that a mesh axis runs over, the one named last changes fastest.
Arguments:
- inputs: bfloat16 [106496, 8192], P('dp', 'mp'), may hold values from -16 to 16
- out_grad: bfloat16 [106496, 512], P('dp'), may hold values from -0.018310547 to 0.018310547
- weight: float32 [8192, 512], P(('mp', 'dp')), may hold values from -8 to 8
- row_moment: float32 [8192], P(('mp', 'dp')), may hold values from 0.015 to 1.5
- col_moment: float32 [512], replicated, may hold values from 0.03 to 1
Outputs:
- new_weight: float32 [8192, 512], P(('mp', 'dp'))
- new_rows: float32 [8192], P(('mp', 'dp'))
- new_cols: float32 [512], replicated
The draws below stay inside these ranges and needn't reach their ends.
All inputs are finite; a program needn't handle non-finite values.
Results may differ from the reference program's by a relative error of at most 0.0003.
Values sent between devices are 32-bit elements; how exact they have to be, the bound alone decides.
No kernel may reach another device: no remote copies, remote signals or barrier semaphores. Data moves between devices by JAX's collectives and lax.ppermute only.
A program may use at most 64 MiB of HBM per device.

```python
import math
import jax
import jax.numpy as jnp
from jax import lax

D = 8192
KV_WIDTH = 512
TOKENS = 106496


def draw_weight(key, part):
    key = jax.random.fold_in(key, 11)
    first = jax.random.fold_in(key, 0)
    ramp = 0.5 + jnp.arange(D, dtype=jnp.float32) / D
    base = jnp.clip(jax.random.normal(first, (D, KV_WIDTH), jnp.float32), -5.0, 5.0)
    return (base * ramp[:, None]).astype(jnp.float32)


def draw_row_moment(key, part):
    key = jax.random.fold_in(key, 12)
    ramp = 0.5 + jnp.arange(D, dtype=jnp.float32) / D
    levels = jnp.exp(jax.random.uniform(key, (D,), jnp.float32, math.log(0.03), 0.0))
    return (levels * ramp).astype(jnp.float32)


def with_spikes(result, rng, source, target, blocks, factor):
    owner, partner = [(jnp.arange(result.shape[position]) // (result.shape[position] // blocks)).reshape([-1 if axis == position else 1 for axis in range(result.ndim)]) for position in (source, target)]
    chosen = jax.random.permutation(rng, blocks)[partner]
    strong = (owner == chosen) | (owner == (partner + blocks // 2) % blocks)
    return jnp.where(strong, factor * result, result)


def steps_of(key, shape, shards, smallest, largest):
    factor_of = 1.0
    for axis_at, parts in shards:
        steps = jax.random.uniform(jax.random.fold_in(jax.random.fold_in(key, 6), axis_at), (parts,), jnp.float32, smallest / len(shards), largest / len(shards))
        factor_of = factor_of * jnp.repeat(jnp.exp(steps), shape[axis_at] // parts).reshape((-1,) + (1,) * (len(shape) - 1 - axis_at))
    return factor_of


def bell_draw(key, dims, width, most, shards=(), kind=jnp.bfloat16):
    drawn = jax.random.normal(key, dims, jnp.float32) * width
    if len(shards) > 0:
        drawn = steps_of(key, dims, shards, -0.22, 0.18) * drawn
    return jnp.clip(drawn, min=-most, max=most).astype(kind)


def noise_with(key, shape, deviation, bound, cuts, heavy, held_as=jnp.bfloat16):
    drawn = deviation * jax.random.normal(key, shape, jnp.float32)
    if cuts:
        drawn = drawn * steps_of(key, shape, cuts, -0.22, 0.18)
    return jnp.clip(with_spikes(drawn, jax.random.fold_in(key, 3), *heavy), -bound, bound).astype(held_as)


def setup_inputs(seed: int = 0) -> dict:
    seeds = jax.random.split(jax.random.key(seed), 6)
    inputs = noise_with(seeds[0], (TOKENS, D), 1.0, 16.0, ((0, 64), (1, 8)), (0, 1, 64, 4.0))
    out_grad = bell_draw(seeds[1], (TOKENS, KV_WIDTH), (TOKENS ** -0.5), 0.018310547, ((0, 64),))
    weight = draw_weight(jax.random.fold_in(seeds[5], 71), 0)
    row_moment = draw_row_moment(jax.random.fold_in(seeds[5], 71), 0)
    col_moment = jnp.clip(jnp.exp(jax.random.uniform(seeds[4], (KV_WIDTH,), jnp.float32, math.log(0.03), math.log(1.0))), 0.03, 1.0)
    return dict(inputs=inputs, out_grad=out_grad, weight=weight, row_moment=row_moment, col_moment=col_moment)


def reference(inputs, out_grad, weight, row_moment, col_moment):
    grad = lax.dot_general(inputs, out_grad, (((0,), (0,)), ((), ())), preferred_element_type=jnp.float32)
    squares = grad * grad
    new_rows = 0.9 * row_moment + 0.1 * lax.optimization_barrier(jnp.mean(squares, axis=1))
    new_cols = 0.9 * col_moment + 0.1 * lax.optimization_barrier(jnp.mean(squares, axis=0))
    row_mean = jnp.mean(new_rows)
    update = grad * lax.rsqrt(new_rows[:, None] * new_cols[None, :] / row_mean)
    update_rms = jnp.sqrt(jnp.mean(update * update))
    weight_rms = jnp.sqrt(jnp.mean(weight * weight) + 1e-06)
    factor = 0.05 * weight_rms / jnp.maximum(jnp.float32(1.0), update_rms)
    new_weight = weight - factor * update
    return (new_weight, new_rows, new_cols)
```

```python
import jax
import jax.numpy as jnp
from jax import lax
from jax.sharding import Mesh, PartitionSpec as P

D = 8192
AXES = ("yh", "x", "z", "yl", "c")
SIZES = (2, 4, 8, 4, 2)
DP = ("yh", "x", "z")
MP = ("yl", "c")


def token_product(inputs, columns):
    return lax.dot_general(
        inputs, columns, (((0,), (0,)), ((), ())), preferred_element_type=jnp.float32
    )


def spread_sum(value, axes, count):
    copies = jnp.broadcast_to(value[None], (count,) + value.shape)
    return jnp.sum(lax.all_to_all(copies, axes, 0, 0, tiled=True), axis=0)


def body(inputs, out_grad, weight, row_moment, col_moment):
    width = out_grad.shape[1]
    parts = token_product(inputs, out_grad).reshape(64, 16, width)
    grad = jnp.sum(lax.all_to_all(parts, DP, 0, 0, tiled=True), axis=0)
    squares = grad * grad
    new_rows = 0.9 * row_moment + 0.1 * jnp.mean(squares, axis=1)
    entries = D * width
    column_part = jnp.sum(squares, axis=0)
    scaled_part = jnp.sum(squares * (1.0 / new_rows)[:, None], axis=0)
    scalars = jnp.concatenate(
        [
            jnp.full((64,), jnp.sum(new_rows)),
            jnp.full((64,), jnp.sum(weight * weight)),
        ]
    )
    small = jnp.concatenate([column_part, scaled_part, scalars])[None]
    small = spread_sum(small, ("x", "z"), 32)
    small = spread_sum(small, ("yh", "yl", "c"), 16)[0]
    column_sum, scaled_sum = small[:width], small[width : 2 * width]
    row_total, weight_total = small[2 * width], small[2 * width + 64]
    new_cols = 0.9 * col_moment + 0.1 * (column_sum / D)
    row_mean = row_total / D
    update_total = row_mean * jnp.sum(scaled_sum / new_cols)
    update = grad * lax.rsqrt(new_rows[:, None] * new_cols[None, :] / row_mean)
    update_rms = jnp.sqrt(update_total / entries)
    weight_rms = jnp.sqrt(weight_total / entries + 1e-06)
    factor = 0.05 * weight_rms / jnp.maximum(jnp.float32(1.0), update_rms)
    new_weight = weight - factor * update
    return (new_weight, new_rows, new_cols)


def solution(mesh):
    fine = Mesh(mesh.devices.reshape(SIZES), AXES)
    placed = (P(DP, MP), P(DP, None), P(MP + DP, None), P(MP + DP), P())
    return jax.shard_map(
        body,
        mesh=fine,
        in_specs=placed,
        out_specs=(P(MP + DP, None), P(MP + DP), P()),
        check_vma=False,
    )
```

```python
import jax
import jax.numpy as jnp
from jax import lax
from jax.experimental import pallas as pl
from jax.experimental.pallas import tpu as pltpu
from jax.sharding import Mesh, PartitionSpec as P

D = 8192
WIDTH = 512
ROWS = 16
LANES = 128
MIB = 1024 * 1024
AXES = ("yh", "x", "z", "yl", "c")
SIZES = (2, 4, 8, 4, 2)
DP = ("yh", "x", "z")
MP = ("yl", "c")
SMALL = 2 * WIDTH + 2 * LANES


def place(yh, x, z, yl, c):
    return (((yh * 4 + x % 4) * 8 + z % 8) * 4 + yl) * 2 + c


def near_groups():
    groups = []
    for yh in range(2):
        for yl in range(4):
            for c in range(2):
                for x in range(c, 4 + c, 2):
                    for z in range(c, 8 + c, 2):
                        groups.append(
                            [place(yh, x + (px + c) % 2, z + (pz + c) % 2, yl, c) for px in range(2) for pz in range(2)]
                        )
    return groups


def far_groups():
    return [
        [place(yh, 2 * x + px, 2 * z + pz, yl, c) for yh in range(2) for x in range(2) for z in range(4)]
        for px in range(2)
        for pz in range(2)
        for yl in range(4)
        for c in range(2)
    ]


def product_kernel(inputs_ref, columns_ref, out_ref):
    product = lax.dot_general(
        inputs_ref[...], columns_ref[...], (((0,), (0,)), ((), ())), preferred_element_type=jnp.float32
    )
    for px in range(2):
        for z in range(4):
            for pz in range(2):
                first = (px * 8 + z * 2 + pz) * ROWS
                out_ref[px * 2 + pz, z] = product[first : first + ROWS]


def token_product(inputs, out_grad):
    tokens, rows = inputs.shape
    return pl.pallas_call(
        product_kernel,
        grid=(4,),
        in_specs=[
            pl.BlockSpec((tokens, rows // 4), lambda i: (0, i)),
            pl.BlockSpec((tokens, WIDTH), lambda i: (0, 0)),
        ],
        out_specs=pl.BlockSpec((4, 4, ROWS, WIDTH), lambda i: (0, i, 0, 0)),
        out_shape=jax.ShapeDtypeStruct((4, 16, ROWS, WIDTH), jnp.float32),
        compiler_params=pltpu.CompilerParams(vmem_limit_bytes=56 * MIB),
    )(inputs, out_grad)


def diagonal():
    return lax.broadcasted_iota(jnp.int32, (ROWS, ROWS), 0) == lax.broadcasted_iota(jnp.int32, (ROWS, ROWS), 1)


def to_column(row):
    return jnp.sum(jnp.where(diagonal(), row, 0.0), axis=1, keepdims=True)


def to_row(column):
    return jnp.sum(jnp.where(diagonal(), column, 0.0), axis=0, keepdims=True)


def statistics_kernel(parts_ref, weight_ref, row_moment_ref, grad_ref, rows_ref, small_ref):
    grad = jnp.sum(parts_ref[...], axis=0)
    grad_ref[...] = grad
    squares = grad * grad
    new_rows = 0.9 * to_column(row_moment_ref[...]) + 0.1 * (jnp.sum(squares, axis=1, keepdims=True) / WIDTH)
    flat_rows = to_row(new_rows)
    rows_ref[...] = flat_rows
    weight_squares = jnp.sum(weight_ref[...] * weight_ref[...], axis=0, keepdims=True)
    small_ref[:, :WIDTH] = jnp.sum(squares, axis=0, keepdims=True)
    small_ref[:, WIDTH : 2 * WIDTH] = jnp.sum(squares / new_rows, axis=0, keepdims=True)
    small_ref[:, 2 * WIDTH : 2 * WIDTH + LANES] = sum(
        weight_squares[:, i : i + LANES] for i in range(0, WIDTH, LANES)
    )
    small_ref[:, 2 * WIDTH + LANES :] = jnp.zeros((1, LANES), jnp.float32)
    small_ref[:, 2 * WIDTH + LANES : 2 * WIDTH + LANES + ROWS] = flat_rows


def statistics(parts, weight, row_moment):
    return pl.pallas_call(
        statistics_kernel,
        out_shape=(
            jax.ShapeDtypeStruct((ROWS, WIDTH), jnp.float32),
            jax.ShapeDtypeStruct((1, ROWS), jnp.float32),
            jax.ShapeDtypeStruct((1, SMALL), jnp.float32),
        ),
    )(parts, weight, row_moment)


def update_kernel(small_ref, grad_ref, rows_ref, weight_ref, col_moment_ref, new_weight_ref, new_cols_ref):
    small = jnp.sum(small_ref[...], axis=0)
    column_sum, scaled_sum = small[:, :WIDTH], small[:, WIDTH : 2 * WIDTH]
    weight_total = jnp.sum(small[:, 2 * WIDTH : 2 * WIDTH + LANES], axis=1, keepdims=True)
    row_mean = jnp.sum(small[:, 2 * WIDTH + LANES :], axis=1, keepdims=True) / D
    new_cols = 0.9 * col_moment_ref[...] + 0.1 * (column_sum / D)
    new_cols_ref[...] = new_cols
    update_total = row_mean * jnp.sum(scaled_sum / new_cols, axis=1, keepdims=True)
    new_rows = to_column(rows_ref[...])
    update = grad_ref[...] * lax.rsqrt(new_rows * new_cols / row_mean)
    entries = D * WIDTH
    update_rms = jnp.sqrt(update_total / entries)
    weight_rms = jnp.sqrt(weight_total / entries + 1e-06)
    factor = 0.05 * weight_rms / jnp.maximum(jnp.float32(1.0), update_rms)
    new_weight_ref[...] = weight_ref[...] - factor * update


def apply_update(small, grad, new_rows, weight, col_moment):
    return pl.pallas_call(
        update_kernel,
        out_shape=(
            jax.ShapeDtypeStruct((ROWS, WIDTH), jnp.float32),
            jax.ShapeDtypeStruct((1, WIDTH), jnp.float32),
        ),
    )(small, grad, new_rows, weight, col_moment)


def copies_of(value, axes, count):
    return lax.all_to_all(jnp.broadcast_to(value[None], (count,) + value.shape), axes, 0, 0, tiled=True)


def body(inputs, out_grad, weight, row_moment, col_moment):
    parts = token_product(inputs, out_grad)
    parts = lax.all_to_all(parts, AXES, 0, 0, tiled=True, axis_index_groups=near_groups())
    parts = jnp.sum(parts, axis=0)
    parts = lax.all_to_all(parts, AXES, 0, 0, tiled=True, axis_index_groups=far_groups())
    grad, new_rows, small = statistics(parts, weight, row_moment.reshape(1, ROWS))
    small = jnp.sum(copies_of(small, ("x", "z"), 32), axis=0)
    small = copies_of(small, ("yh", "yl", "c"), 16)
    new_weight, new_cols = apply_update(small, grad, new_rows, weight, col_moment.reshape(1, WIDTH))
    return (new_weight, new_rows.reshape(ROWS), new_cols.reshape(WIDTH))


def solution(mesh):
    fine = Mesh(mesh.devices.reshape(SIZES), AXES)
    placed = (P(DP, MP), P(DP, None), P(MP + DP, None), P(MP + DP), P())
    return jax.shard_map(
        body,
        mesh=fine,
        in_specs=placed,
        out_specs=(P(MP + DP, None), P(MP + DP), P()),
        check_vma=False,
    )
```

```python
import jax
import jax.numpy as jnp
from jax import lax
from jax.experimental import pallas as pl
from jax.experimental.pallas import tpu as pltpu
from jax.sharding import Mesh, PartitionSpec as P

D = 8192
WIDTH = 512
ROWS = 16
LANES = 128
MIB = 1024 * 1024
AXES = ("yh", "x", "z", "yl", "c")
SIZES = (2, 4, 8, 4, 2)
DP = ("yh", "x", "z")
MP = ("yl", "c")
SMALL = 2 * WIDTH + 2 * LANES


def place(yh, x, z, yl, c):
    return (((yh * 4 + x % 4) * 8 + z % 8) * 4 + yl) * 2 + c


def near_groups():
    groups = []
    for yh in range(2):
        for yl in range(4):
            for c in range(2):
                for x in range(c, 4 + c, 2):
                    for z in range(c, 8 + c, 2):
                        groups.append(
                            [place(yh, x + (px + c) % 2, z + (pz + c) % 2, yl, c) for px in range(2) for pz in range(2)]
                        )
    return groups


def far_groups():
    return [
        [place(yh, 2 * x + px, 2 * z + pz, yl, c) for yh in range(2) for x in range(2) for z in range(4)]
        for px in range(2)
        for pz in range(2)
        for yl in range(4)
        for c in range(2)
    ]


CHUNKS = (512, 512, 640)
BLOCKS = 4


def product_kernel(inputs_ref, columns_ref, out_ref, inputs, columns, total, ordered, in_sems, column_sems, out_sems):
    copies = []
    first = 0
    for i, tokens in enumerate(CHUNKS):
        span = pl.ds(first, tokens)
        pair = (
            pltpu.make_async_copy(columns_ref.at[span], columns.at[span], column_sems.at[i]),
            pltpu.make_async_copy(inputs_ref.at[span], inputs.at[span], in_sems.at[i]),
        )
        for copy in pair:
            copy.start()
        copies.append((first, tokens, pair))
        first += tokens
    size = inputs.shape[1] // BLOCKS
    writes = []
    for i, (first, tokens, pair) in enumerate(copies):
        for copy in pair:
            copy.wait()
        for block in range(BLOCKS):
            rows = slice(block * size, (block + 1) * size)
            product = lax.dot_general(
                inputs[first : first + tokens, rows],
                columns[first : first + tokens],
                (((0,), (0,)), ((), ())),
                preferred_element_type=jnp.float32,
            )
            if i > 0:
                product = product + total[rows]
            if i < len(CHUNKS) - 1:
                total[rows] = product
                continue
            for px in range(2):
                for z in range(4):
                    for pz in range(2):
                        row = (px * 8 + z * 2 + pz) * ROWS
                        ordered[px * 2 + pz, 4 * block + z] = product[row : row + ROWS]
            place_of = pl.ds(4 * block, 4)
            write = pltpu.make_async_copy(ordered.at[:, place_of], out_ref.at[:, place_of], out_sems.at[block])
            write.start()
            writes.append(write)
    for write in writes:
        write.wait()


def token_product(inputs, out_grad):
    tokens, rows = inputs.shape
    ordered = (4, 16, ROWS, WIDTH)
    return pl.pallas_call(
        product_kernel,
        in_specs=[pl.BlockSpec(memory_space=pl.ANY)] * 2,
        out_specs=pl.BlockSpec(memory_space=pl.ANY),
        out_shape=jax.ShapeDtypeStruct(ordered, jnp.float32),
        scratch_shapes=[
            pltpu.VMEM((tokens, rows), jnp.bfloat16),
            pltpu.VMEM((tokens, WIDTH), jnp.bfloat16),
            pltpu.VMEM((rows, WIDTH), jnp.float32),
            pltpu.VMEM(ordered, jnp.float32),
            pltpu.SemaphoreType.DMA((len(CHUNKS),)),
            pltpu.SemaphoreType.DMA((len(CHUNKS),)),
            pltpu.SemaphoreType.DMA((BLOCKS,)),
        ],
        compiler_params=pltpu.CompilerParams(vmem_limit_bytes=57 * MIB),
    )(inputs, out_grad)


def diagonal():
    return lax.broadcasted_iota(jnp.int32, (ROWS, ROWS), 0) == lax.broadcasted_iota(jnp.int32, (ROWS, ROWS), 1)


def to_column(row):
    return jnp.sum(jnp.where(diagonal(), row, 0.0), axis=1, keepdims=True)


def to_row(column):
    return jnp.sum(jnp.where(diagonal(), column, 0.0), axis=0, keepdims=True)


def statistics_kernel(parts_ref, weight_ref, row_moment_ref, grad_ref, rows_ref, small_ref):
    grad = jnp.sum(parts_ref[...], axis=0)
    grad_ref[...] = grad
    squares = grad * grad
    new_rows = 0.9 * to_column(row_moment_ref[...]) + 0.1 * (jnp.sum(squares, axis=1, keepdims=True) / WIDTH)
    flat_rows = to_row(new_rows)
    rows_ref[...] = flat_rows
    weight_squares = jnp.sum(weight_ref[...] * weight_ref[...], axis=0, keepdims=True)
    small_ref[:, :WIDTH] = jnp.sum(squares, axis=0, keepdims=True)
    small_ref[:, WIDTH : 2 * WIDTH] = jnp.sum(squares / new_rows, axis=0, keepdims=True)
    small_ref[:, 2 * WIDTH : 2 * WIDTH + LANES] = sum(
        weight_squares[:, i : i + LANES] for i in range(0, WIDTH, LANES)
    )
    small_ref[:, 2 * WIDTH + LANES :] = jnp.zeros((1, LANES), jnp.float32)
    small_ref[:, 2 * WIDTH + LANES : 2 * WIDTH + LANES + ROWS] = flat_rows


def statistics(parts, weight, row_moment):
    return pl.pallas_call(
        statistics_kernel,
        out_shape=(
            jax.ShapeDtypeStruct((ROWS, WIDTH), jnp.float32),
            jax.ShapeDtypeStruct((1, ROWS), jnp.float32),
            jax.ShapeDtypeStruct((1, SMALL), jnp.float32),
        ),
    )(parts, weight, row_moment)


def update_kernel(small_ref, grad_ref, rows_ref, weight_ref, col_moment_ref, new_weight_ref, new_rows_ref, new_cols_ref):
    new_rows_ref[...] = rows_ref[...]
    small = jnp.sum(small_ref[...], axis=0)
    column_sum, scaled_sum = small[:, :WIDTH], small[:, WIDTH : 2 * WIDTH]
    weight_total = jnp.sum(small[:, 2 * WIDTH : 2 * WIDTH + LANES], axis=1, keepdims=True)
    row_mean = jnp.sum(small[:, 2 * WIDTH + LANES :], axis=1, keepdims=True) / D
    new_cols = 0.9 * col_moment_ref[...] + 0.1 * (column_sum / D)
    new_cols_ref[...] = new_cols
    update_total = row_mean * jnp.sum(scaled_sum / new_cols, axis=1, keepdims=True)
    new_rows = to_column(rows_ref[...])
    update = grad_ref[...] * lax.rsqrt(new_rows * new_cols / row_mean)
    entries = D * WIDTH
    update_rms = jnp.sqrt(update_total / entries)
    weight_rms = jnp.sqrt(weight_total / entries + 1e-06)
    factor = 0.05 * weight_rms / jnp.maximum(jnp.float32(1.0), update_rms)
    new_weight_ref[...] = weight_ref[...] - factor * update


def apply_update(small, grad, new_rows, weight, col_moment):
    return pl.pallas_call(
        update_kernel,
        out_shape=(
            jax.ShapeDtypeStruct((ROWS, WIDTH), jnp.float32),
            jax.ShapeDtypeStruct((1, ROWS), jnp.float32),
            jax.ShapeDtypeStruct((1, WIDTH), jnp.float32),
        ),
    )(small, grad, new_rows, weight, col_moment)


def copies_of(value, axes, count):
    return lax.all_to_all(jnp.broadcast_to(value[None], (count,) + value.shape), axes, 0, 0, tiled=True)


def body(inputs, out_grad, weight, row_moment, col_moment):
    parts = token_product(inputs, out_grad)
    parts = lax.all_to_all(parts, AXES, 0, 0, tiled=True, axis_index_groups=near_groups())
    parts = jnp.sum(parts, axis=0)
    parts = lax.all_to_all(parts, AXES, 0, 0, tiled=True, axis_index_groups=far_groups())
    grad, row_values, small = statistics(parts, weight, row_moment.reshape(1, ROWS))
    small = jnp.sum(copies_of(small, ("x", "z"), 32), axis=0)
    small = copies_of(small, ("yh", "yl", "c"), 16)
    new_weight, new_rows, new_cols = apply_update(small, grad, row_values, weight, col_moment.reshape(1, WIDTH))
    return (new_weight, new_rows.reshape(ROWS), new_cols.reshape(WIDTH))


def solution(mesh):
    fine = Mesh(mesh.devices.reshape(SIZES), AXES)
    placed = (P(DP, MP), P(DP, None), P(MP + DP, None), P(MP + DP), P())
    return jax.shard_map(
        body,
        mesh=fine,
        in_specs=placed,
        out_specs=(P(MP + DP, None), P(MP + DP), P()),
        check_vma=False,
    )
```

```python
import jax
import jax.numpy as jnp
from jax import lax
from jax.experimental import pallas as pl
from jax.experimental.pallas import tpu as pltpu
from jax.sharding import Mesh, PartitionSpec as P

D = 8192
WIDTH = 512
ROWS = 16
LANES = 128
MIB = 1024 * 1024
AXES = ("yh", "x", "z", "yl", "c")
SIZES = (2, 4, 8, 4, 2)
DP = ("yh", "x", "z")
MP = ("yl", "c")
SMALL = 2 * WIDTH + 2 * LANES


def place(yh, x, z, yl, c):
    return (((yh * 4 + x % 4) * 8 + z % 8) * 4 + yl) * 2 + c


def near_groups():
    groups = []
    for yh in range(2):
        for yl in range(4):
            for c in range(2):
                for x in range(c, 4 + c, 2):
                    for z in range(c, 8 + c, 2):
                        groups.append(
                            [place(yh, x + (px + c) % 2, z + (pz + c) % 2, yl, c) for px in range(2) for pz in range(2)]
                        )
    return groups


def far_groups():
    return [
        [place(yh, 2 * x + px, 2 * z + pz, yl, c) for yh in range(2) for x in range(2) for z in range(4)]
        for px in range(2)
        for pz in range(2)
        for yl in range(4)
        for c in range(2)
    ]


CHUNKS = (512, 512, 640)
BLOCKS = 4
HERE = pl.BlockSpec(memory_space=pltpu.VMEM)


def in_vmem(array):
    return pltpu.with_memory_space_constraint(array, pltpu.VMEM)


def in_hbm(array):
    return pltpu.with_memory_space_constraint(array, pltpu.HBM)


def product_kernel(inputs_ref, columns_ref, out_ref, inputs, columns, total, in_sems, column_sems):
    copies = []
    first = 0
    for i, tokens in enumerate(CHUNKS):
        span = pl.ds(first, tokens)
        pair = (
            pltpu.make_async_copy(columns_ref.at[span], columns.at[span], column_sems.at[i]),
            pltpu.make_async_copy(inputs_ref.at[span], inputs.at[span], in_sems.at[i]),
        )
        for copy in pair:
            copy.start()
        copies.append((first, tokens, pair))
        first += tokens
    size = inputs.shape[1] // BLOCKS
    for i, (first, tokens, pair) in enumerate(copies):
        for copy in pair:
            copy.wait()
        for block in range(BLOCKS):
            rows = slice(block * size, (block + 1) * size)
            product = lax.dot_general(
                inputs[first : first + tokens, rows],
                columns[first : first + tokens],
                (((0,), (0,)), ((), ())),
                preferred_element_type=jnp.float32,
            )
            if i > 0:
                product = product + total[rows]
            if i < len(CHUNKS) - 1:
                total[rows] = product
                continue
            for px in range(2):
                for z in range(4):
                    for pz in range(2):
                        row = (px * 8 + z * 2 + pz) * ROWS
                        out_ref[px * 2 + pz, 4 * block + z] = product[row : row + ROWS]


def token_product(inputs, out_grad):
    tokens, rows = inputs.shape
    return pl.pallas_call(
        product_kernel,
        in_specs=[pl.BlockSpec(memory_space=pl.ANY)] * 2,
        out_specs=HERE,
        out_shape=pltpu.VMEM((4, 16, ROWS, WIDTH), jnp.float32),
        scratch_shapes=[
            pltpu.VMEM((tokens, rows), jnp.bfloat16),
            pltpu.VMEM((tokens, WIDTH), jnp.bfloat16),
            pltpu.VMEM((rows, WIDTH), jnp.float32),
            pltpu.SemaphoreType.DMA((len(CHUNKS),)),
            pltpu.SemaphoreType.DMA((len(CHUNKS),)),
        ],
        compiler_params=pltpu.CompilerParams(vmem_limit_bytes=24 * MIB),
    )(in_hbm(inputs), in_hbm(out_grad))


def diagonal():
    return lax.broadcasted_iota(jnp.int32, (ROWS, ROWS), 0) == lax.broadcasted_iota(jnp.int32, (ROWS, ROWS), 1)


def to_column(row):
    return jnp.sum(jnp.where(diagonal(), row, 0.0), axis=1, keepdims=True)


def to_row(column):
    return jnp.sum(jnp.where(diagonal(), column, 0.0), axis=0, keepdims=True)


def statistics_kernel(parts_ref, weight_ref, row_moment_ref, grad_ref, rows_ref, small_ref):
    grad = jnp.sum(parts_ref[...], axis=0)
    grad_ref[...] = grad
    squares = grad * grad
    new_rows = 0.9 * to_column(row_moment_ref[...]) + 0.1 * (jnp.sum(squares, axis=1, keepdims=True) / WIDTH)
    flat_rows = to_row(new_rows)
    rows_ref[...] = flat_rows
    weight_squares = jnp.sum(weight_ref[...] * weight_ref[...], axis=0, keepdims=True)
    small_ref[:, :WIDTH] = jnp.sum(squares, axis=0, keepdims=True)
    small_ref[:, WIDTH : 2 * WIDTH] = jnp.sum(squares / new_rows, axis=0, keepdims=True)
    small_ref[:, 2 * WIDTH : 2 * WIDTH + LANES] = sum(
        weight_squares[:, i : i + LANES] for i in range(0, WIDTH, LANES)
    )
    small_ref[:, 2 * WIDTH + LANES :] = jnp.zeros((1, LANES), jnp.float32)
    small_ref[:, 2 * WIDTH + LANES : 2 * WIDTH + LANES + ROWS] = flat_rows


def statistics(parts, weight, row_moment):
    return pl.pallas_call(
        statistics_kernel,
        in_specs=[HERE] * 3,
        out_specs=(HERE,) * 3,
        out_shape=(
            pltpu.VMEM((ROWS, WIDTH), jnp.float32),
            pltpu.VMEM((1, ROWS), jnp.float32),
            pltpu.VMEM((1, SMALL), jnp.float32),
        ),
    )(in_vmem(parts), in_vmem(weight), in_vmem(row_moment))


def update_kernel(small_ref, grad_ref, rows_ref, weight_ref, col_moment_ref, new_weight_ref, new_rows_ref, new_cols_ref):
    new_rows_ref[...] = rows_ref[...]
    small = jnp.sum(small_ref[...], axis=0)
    column_sum, scaled_sum = small[:, :WIDTH], small[:, WIDTH : 2 * WIDTH]
    weight_total = jnp.sum(small[:, 2 * WIDTH : 2 * WIDTH + LANES], axis=1, keepdims=True)
    row_mean = jnp.sum(small[:, 2 * WIDTH + LANES :], axis=1, keepdims=True) / D
    new_cols = 0.9 * col_moment_ref[...] + 0.1 * (column_sum / D)
    new_cols_ref[...] = new_cols
    update_total = row_mean * jnp.sum(scaled_sum / new_cols, axis=1, keepdims=True)
    new_rows = to_column(rows_ref[...])
    update = grad_ref[...] * lax.rsqrt(new_rows * new_cols / row_mean)
    entries = D * WIDTH
    update_rms = jnp.sqrt(update_total / entries)
    weight_rms = jnp.sqrt(weight_total / entries + 1e-06)
    factor = 0.05 * weight_rms / jnp.maximum(jnp.float32(1.0), update_rms)
    new_weight_ref[...] = weight_ref[...] - factor * update


def apply_update(small, grad, new_rows, weight, col_moment):
    return pl.pallas_call(
        update_kernel,
        in_specs=[HERE] * 5,
        out_specs=(HERE,) * 3,
        out_shape=(
            jax.ShapeDtypeStruct((ROWS, WIDTH), jnp.float32),
            jax.ShapeDtypeStruct((1, ROWS), jnp.float32),
            jax.ShapeDtypeStruct((1, WIDTH), jnp.float32),
        ),
    )(*(in_vmem(array) for array in (small, grad, new_rows, weight, col_moment)))


def copies_of(value, axes, count):
    return lax.all_to_all(jnp.broadcast_to(value[None], (count,) + value.shape), axes, 0, 0, tiled=True)


def body(inputs, out_grad, weight, row_moment, col_moment):
    parts = token_product(inputs, out_grad)
    parts = lax.all_to_all(parts, AXES, 0, 0, tiled=True, axis_index_groups=near_groups())
    parts = jnp.sum(parts, axis=0)
    parts = lax.all_to_all(parts, AXES, 0, 0, tiled=True, axis_index_groups=far_groups())
    grad, row_values, small = statistics(parts, weight, row_moment.reshape(1, ROWS))
    small = jnp.sum(copies_of(small, ("x", "z"), 32), axis=0)
    small = copies_of(small, ("yh", "yl", "c"), 16)
    new_weight, new_rows, new_cols = apply_update(small, grad, row_values, weight, col_moment.reshape(1, WIDTH))
    return (new_weight, new_rows.reshape(ROWS), new_cols.reshape(WIDTH))


def solution(mesh):
    fine = Mesh(mesh.devices.reshape(SIZES), AXES)
    placed = (P(DP, MP), P(DP, None), P(MP + DP, None), P(MP + DP), P())
    return jax.shard_map(
        body,
        mesh=fine,
        in_specs=placed,
        out_specs=(P(MP + DP, None), P(MP + DP), P()),
        check_vma=False,
    )
```

```python
import jax
import jax.numpy as jnp
from jax import lax
from jax.experimental import pallas as pl
from jax.experimental.pallas import tpu as pltpu
from jax.sharding import Mesh, PartitionSpec as P

D = 8192
WIDTH = 512
ROWS = 16
LANES = 128
MIB = 1024 * 1024
AXES = ("yh", "x", "z", "yl", "c")
SIZES = (2, 4, 8, 4, 2)
DP = ("yh", "x", "z")
MP = ("yl", "c")
SMALL = 2 * WIDTH + 2 * LANES


def place(yh, x, z, yl, c):
    return (((yh * 4 + x % 4) * 8 + z % 8) * 4 + yl) * 2 + c


def neighbour(index, core, steps):
    return (index + (1 if (index + core) % 2 == 0 else -1)) % steps


def near_pairs(along_x, along_z):
    return [
        (
            place(yh, x, z, yl, c),
            place(yh, neighbour(x, c, 4) if along_x else x, neighbour(z, c, 8) if along_z else z, yl, c),
        )
        for yh in range(2)
        for x in range(4)
        for z in range(8)
        for yl in range(4)
        for c in range(2)
    ]


def far_groups():
    return [
        [place(yh, 2 * x + px, 2 * z + pz, yl, c) for yh in range(2) for x in range(2) for z in range(4)]
        for px in range(2)
        for pz in range(2)
        for yl in range(4)
        for c in range(2)
    ]


CHUNKS = (512, 512, 640)
STRIPE = 128
STRIPES = 4
HERE = pl.BlockSpec(memory_space=pltpu.VMEM)


def in_vmem(array):
    return pltpu.with_memory_space_constraint(array, pltpu.VMEM)


def in_hbm(array):
    return pltpu.with_memory_space_constraint(array, pltpu.HBM)


def by_z_parity(product, parity, same_ref, other_ref):
    for j in range(STRIPES * 4):
        for ref, side in ((same_ref, parity), (other_ref, 1 - parity)):
            row = pl.multiple_of((2 * j + side) * ROWS, ROWS)
            ref[j] = product[pl.ds(row, ROWS), :]


def away_kernel(
    inputs_ref, columns_ref, side_ref, across_ref, kept_ref, columns, inputs, total, column_sems, in_sems, kept_sems
):
    mine = lax.axis_index("x") % 2

    def fetch(source, span, target, stripe, parity, semaphore):
        lanes = pl.ds(pl.multiple_of((2 * stripe + parity) * STRIPE, STRIPE), STRIPE)
        return pltpu.make_async_copy(
            source.at[span, lanes], target.at[span, pl.ds(stripe * STRIPE, STRIPE)], semaphore
        )

    copies = []
    first = 0
    for i, tokens in enumerate(CHUNKS):
        span = pl.ds(first, tokens)
        group = [pltpu.make_async_copy(columns_ref.at[span], columns.at[span], column_sems.at[i])]
        group += [fetch(inputs_ref, span, inputs, s, 1 - mine, in_sems.at[i, s]) for s in range(STRIPES)]
        for copy in group:
            copy.start()
        copies.append((first, tokens, group))
        first += tokens
    kept = [fetch(inputs_ref, pl.ds(0, first), kept_ref, s, mine, kept_sems.at[s]) for s in range(STRIPES)]
    for copy in kept:
        copy.start()
    for i, (first, tokens, group) in enumerate(copies):
        for copy in group:
            copy.wait()
        product = lax.dot_general(
            inputs[first : first + tokens],
            columns[first : first + tokens],
            (((0,), (0,)), ((), ())),
            preferred_element_type=jnp.float32,
        )
        total[...] = product if i == 0 else total[...] + product
    by_z_parity(total, lax.axis_index("z") % 2, side_ref, across_ref)
    for copy in kept:
        copy.wait()


def rest_kernel(kept_ref, columns_ref, own_ref, side_ref, total):
    total[...] = lax.dot_general(
        kept_ref[...], columns_ref[...], (((0,), (0,)), ((), ())), preferred_element_type=jnp.float32
    )
    by_z_parity(total, lax.axis_index("z") % 2, own_ref, side_ref)


def near_sum(inputs, out_grad):
    tokens, rows = inputs.shape
    block = pltpu.VMEM((16, ROWS, WIDTH), jnp.float32)
    half = pltpu.VMEM((tokens, rows // 2), jnp.bfloat16)
    all_columns = pltpu.VMEM((tokens, WIDTH), jnp.bfloat16)
    total = pltpu.VMEM((rows // 2, WIDTH), jnp.float32)
    limit = pltpu.CompilerParams(vmem_limit_bytes=24 * MIB)
    to_x, to_both, kept, columns = pl.pallas_call(
        away_kernel,
        in_specs=[pl.BlockSpec(memory_space=pl.ANY)] * 2,
        out_specs=(HERE,) * 4,
        out_shape=(block, block, half, all_columns),
        scratch_shapes=[
            half,
            total,
            pltpu.SemaphoreType.DMA((len(CHUNKS),)),
            pltpu.SemaphoreType.DMA((len(CHUNKS), STRIPES)),
            pltpu.SemaphoreType.DMA((STRIPES,)),
        ],
        compiler_params=limit,
    )(in_hbm(inputs), in_hbm(out_grad))
    from_both = lax.ppermute(to_both, AXES, near_pairs(True, True))
    from_x = lax.ppermute(to_x, AXES, near_pairs(True, False))
    own, to_z = pl.pallas_call(
        rest_kernel,
        in_specs=[HERE] * 2,
        out_specs=(HERE,) * 2,
        out_shape=(block, block),
        scratch_shapes=[total],
        compiler_params=limit,
    )(in_vmem(kept), in_vmem(columns))
    from_z = lax.ppermute(to_z, AXES, near_pairs(False, True))
    return (own + from_both) + (from_x + from_z)


def diagonal():
    return lax.broadcasted_iota(jnp.int32, (ROWS, ROWS), 0) == lax.broadcasted_iota(jnp.int32, (ROWS, ROWS), 1)


def to_column(row):
    return jnp.sum(jnp.where(diagonal(), row, 0.0), axis=1, keepdims=True)


def to_row(column):
    return jnp.sum(jnp.where(diagonal(), column, 0.0), axis=0, keepdims=True)


def statistics_kernel(parts_ref, weight_ref, row_moment_ref, grad_ref, rows_ref, small_ref):
    grad = jnp.sum(parts_ref[...], axis=0)
    grad_ref[...] = grad
    squares = grad * grad
    new_rows = 0.9 * to_column(row_moment_ref[...]) + 0.1 * (jnp.sum(squares, axis=1, keepdims=True) / WIDTH)
    flat_rows = to_row(new_rows)
    rows_ref[...] = flat_rows
    weight_squares = jnp.sum(weight_ref[...] * weight_ref[...], axis=0, keepdims=True)
    small_ref[:, :WIDTH] = jnp.sum(squares, axis=0, keepdims=True)
    small_ref[:, WIDTH : 2 * WIDTH] = jnp.sum(squares / new_rows, axis=0, keepdims=True)
    small_ref[:, 2 * WIDTH : 2 * WIDTH + LANES] = sum(
        weight_squares[:, i : i + LANES] for i in range(0, WIDTH, LANES)
    )
    small_ref[:, 2 * WIDTH + LANES :] = jnp.zeros((1, LANES), jnp.float32)
    small_ref[:, 2 * WIDTH + LANES : 2 * WIDTH + LANES + ROWS] = flat_rows


def statistics(parts, weight, row_moment):
    return pl.pallas_call(
        statistics_kernel,
        in_specs=[HERE] * 3,
        out_specs=(HERE,) * 3,
        out_shape=(
            pltpu.VMEM((ROWS, WIDTH), jnp.float32),
            pltpu.VMEM((1, ROWS), jnp.float32),
            pltpu.VMEM((1, SMALL), jnp.float32),
        ),
    )(in_vmem(parts), in_vmem(weight), in_vmem(row_moment))


def update_kernel(small_ref, grad_ref, rows_ref, weight_ref, col_moment_ref, new_weight_ref, new_rows_ref, new_cols_ref):
    new_rows_ref[...] = rows_ref[...]
    small = jnp.sum(small_ref[...], axis=0)
    column_sum, scaled_sum = small[:, :WIDTH], small[:, WIDTH : 2 * WIDTH]
    weight_total = jnp.sum(small[:, 2 * WIDTH : 2 * WIDTH + LANES], axis=1, keepdims=True)
    row_mean = jnp.sum(small[:, 2 * WIDTH + LANES :], axis=1, keepdims=True) / D
    new_cols = 0.9 * col_moment_ref[...] + 0.1 * (column_sum / D)
    new_cols_ref[...] = new_cols
    update_total = row_mean * jnp.sum(scaled_sum / new_cols, axis=1, keepdims=True)
    new_rows = to_column(rows_ref[...])
    update = grad_ref[...] * lax.rsqrt(new_rows * new_cols / row_mean)
    entries = D * WIDTH
    update_rms = jnp.sqrt(update_total / entries)
    weight_rms = jnp.sqrt(weight_total / entries + 1e-06)
    factor = 0.05 * weight_rms / jnp.maximum(jnp.float32(1.0), update_rms)
    new_weight_ref[...] = weight_ref[...] - factor * update


def apply_update(small, grad, new_rows, weight, col_moment):
    return pl.pallas_call(
        update_kernel,
        in_specs=[HERE] * 5,
        out_specs=(HERE,) * 3,
        out_shape=(
            jax.ShapeDtypeStruct((ROWS, WIDTH), jnp.float32),
            jax.ShapeDtypeStruct((1, ROWS), jnp.float32),
            jax.ShapeDtypeStruct((1, WIDTH), jnp.float32),
        ),
    )(*(in_vmem(array) for array in (small, grad, new_rows, weight, col_moment)))


def copies_of(value, axes, count):
    return lax.all_to_all(jnp.broadcast_to(value[None], (count,) + value.shape), axes, 0, 0, tiled=True)


def body(inputs, out_grad, weight, row_moment, col_moment):
    parts = near_sum(inputs, out_grad)
    parts = lax.all_to_all(parts, AXES, 0, 0, tiled=True, axis_index_groups=far_groups())
    grad, row_values, small = statistics(parts, weight, row_moment.reshape(1, ROWS))
    small = jnp.sum(copies_of(small, ("x", "z"), 32), axis=0)
    small = copies_of(small, ("yh", "yl", "c"), 16)
    new_weight, new_rows, new_cols = apply_update(small, grad, row_values, weight, col_moment.reshape(1, WIDTH))
    return (new_weight, new_rows.reshape(ROWS), new_cols.reshape(WIDTH))


def solution(mesh):
    fine = Mesh(mesh.devices.reshape(SIZES), AXES)
    placed = (P(DP, MP), P(DP, None), P(MP + DP, None), P(MP + DP), P())
    return jax.shard_map(
        body,
        mesh=fine,
        in_specs=placed,
        out_specs=(P(MP + DP, None), P(MP + DP), P()),
        check_vma=False,
    )
```

```python
import jax
import jax.numpy as jnp
from jax import lax
from jax.experimental import pallas as pl
from jax.experimental.pallas import tpu as pltpu
from jax.sharding import Mesh, PartitionSpec as P

D = 8192
WIDTH = 512
ROWS = 16
LANES = 128
MIB = 1024 * 1024
AXES = ("yh", "x", "z", "yl", "c")
SIZES = (2, 4, 8, 4, 2)
DP = ("yh", "x", "z")
MP = ("yl", "c")
SMALL = 2 * WIDTH + 2 * LANES


CLASS_X = ((1, 2), (0, 3))
CLASS_Z = ((1, 3, 4, 6), (0, 2, 5, 7))
BLOCKS_X = ((0, 1), (2, 3))
BLOCKS_Z = ((0, 1), (2, 3), (4, 5), (6, 7))


def place(yh, x, z, yl, c):
    return (((yh * 4 + (x + c) % 4) * 8 + (z + c) % 8) * 4 + yl) * 2 + c


def near_groups():
    return [
        [
            place(yh, next(x for x in xs if x in class_x), next(z for z in zs if z in class_z), yl, c)
            for class_x in CLASS_X
            for class_z in CLASS_Z
        ]
        for yh in range(2)
        for xs in BLOCKS_X
        for zs in BLOCKS_Z
        for yl in range(4)
        for c in range(2)
    ]


def far_groups():
    return [
        [place(yh, x, z, yl, c) for yh in range(2) for x in class_x for z in class_z]
        for class_x in CLASS_X
        for class_z in CLASS_Z
        for yl in range(4)
        for c in range(2)
    ]


def position(yh, x, z, core):
    x, z = (x - core) % 4, (z - core) % 8
    kx = next(k for k, xs in enumerate(CLASS_X) if x in xs)
    kz = next(k for k, zs in enumerate(CLASS_Z) if z in zs)
    return 2 * kx + kz, (2 * yh + CLASS_X[kx].index(x)) * 4 + CLASS_Z[kz].index(z)


CHUNKS = (512, 512, 640)
BLOCKS = 4
HERE = pl.BlockSpec(memory_space=pltpu.VMEM)


def in_vmem(array):
    return pltpu.with_memory_space_constraint(array, pltpu.VMEM)


def in_hbm(array):
    return pltpu.with_memory_space_constraint(array, pltpu.HBM)


def product_kernel(inputs_ref, columns_ref, out_ref, inputs, columns, total, in_sems, column_sems):
    core = lax.axis_index("c")
    copies = []
    first = 0
    for i, tokens in enumerate(CHUNKS):
        span = pl.ds(first, tokens)
        pair = (
            pltpu.make_async_copy(columns_ref.at[span], columns.at[span], column_sems.at[i]),
            pltpu.make_async_copy(inputs_ref.at[span], inputs.at[span], in_sems.at[i]),
        )
        for copy in pair:
            copy.start()
        copies.append((first, tokens, pair))
        first += tokens
    size = inputs.shape[1] // BLOCKS
    for i, (first, tokens, pair) in enumerate(copies):
        for copy in pair:
            copy.wait()
        for block in range(BLOCKS):
            rows = slice(block * size, (block + 1) * size)
            product = lax.dot_general(
                inputs[first : first + tokens, rows],
                columns[first : first + tokens],
                (((0,), (0,)), ((), ())),
                preferred_element_type=jnp.float32,
            )
            if i > 0:
                product = product + total[rows]
            if i < len(CHUNKS) - 1:
                total[rows] = product
                continue
            for r in range(size // ROWS):
                device = block * (size // ROWS) + r
                where = device // 32, device // 8 % 4, device % 8
                (kind, index), (kind1, index1) = position(*where, 0), position(*where, 1)
                kind, index = kind + core * (kind1 - kind), index + core * (index1 - index)
                out_ref[kind, index] = product[r * ROWS : (r + 1) * ROWS]


def token_product(inputs, out_grad):
    tokens, rows = inputs.shape
    return pl.pallas_call(
        product_kernel,
        in_specs=[pl.BlockSpec(memory_space=pl.ANY)] * 2,
        out_specs=HERE,
        out_shape=pltpu.VMEM((4, 16, ROWS, WIDTH), jnp.float32),
        scratch_shapes=[
            pltpu.VMEM((tokens, rows), jnp.bfloat16),
            pltpu.VMEM((tokens, WIDTH), jnp.bfloat16),
            pltpu.VMEM((rows, WIDTH), jnp.float32),
            pltpu.SemaphoreType.DMA((len(CHUNKS),)),
            pltpu.SemaphoreType.DMA((len(CHUNKS),)),
        ],
        compiler_params=pltpu.CompilerParams(vmem_limit_bytes=24 * MIB),
    )(in_hbm(inputs), in_hbm(out_grad))


def diagonal():
    return lax.broadcasted_iota(jnp.int32, (ROWS, ROWS), 0) == lax.broadcasted_iota(jnp.int32, (ROWS, ROWS), 1)


def to_column(row):
    return jnp.sum(jnp.where(diagonal(), row, 0.0), axis=1, keepdims=True)


def to_row(column):
    return jnp.sum(jnp.where(diagonal(), column, 0.0), axis=0, keepdims=True)


def statistics_kernel(parts_ref, weight_ref, row_moment_ref, grad_ref, rows_ref, small_ref):
    grad = jnp.sum(parts_ref[...], axis=0)
    grad_ref[...] = grad
    squares = grad * grad
    new_rows = 0.9 * to_column(row_moment_ref[...]) + 0.1 * (jnp.sum(squares, axis=1, keepdims=True) / WIDTH)
    flat_rows = to_row(new_rows)
    rows_ref[...] = flat_rows
    weight_squares = jnp.sum(weight_ref[...] * weight_ref[...], axis=0, keepdims=True)
    small_ref[:, :WIDTH] = jnp.sum(squares, axis=0, keepdims=True)
    small_ref[:, WIDTH : 2 * WIDTH] = jnp.sum(squares / new_rows, axis=0, keepdims=True)
    small_ref[:, 2 * WIDTH : 2 * WIDTH + LANES] = sum(
        weight_squares[:, i : i + LANES] for i in range(0, WIDTH, LANES)
    )
    small_ref[:, 2 * WIDTH + LANES :] = jnp.zeros((1, LANES), jnp.float32)
    small_ref[:, 2 * WIDTH + LANES : 2 * WIDTH + LANES + ROWS] = flat_rows


def statistics(parts, weight, row_moment):
    return pl.pallas_call(
        statistics_kernel,
        in_specs=[HERE] * 3,
        out_specs=(HERE,) * 3,
        out_shape=(
            pltpu.VMEM((ROWS, WIDTH), jnp.float32),
            pltpu.VMEM((1, ROWS), jnp.float32),
            pltpu.VMEM((1, SMALL), jnp.float32),
        ),
    )(in_vmem(parts), in_vmem(weight), in_vmem(row_moment))


def update_kernel(small_ref, grad_ref, rows_ref, weight_ref, col_moment_ref, new_weight_ref, new_rows_ref, new_cols_ref):
    new_rows_ref[...] = rows_ref[...]
    small = jnp.sum(small_ref[...], axis=0)
    column_sum, scaled_sum = small[:, :WIDTH], small[:, WIDTH : 2 * WIDTH]
    weight_total = jnp.sum(small[:, 2 * WIDTH : 2 * WIDTH + LANES], axis=1, keepdims=True)
    row_mean = jnp.sum(small[:, 2 * WIDTH + LANES :], axis=1, keepdims=True) / D
    new_cols = 0.9 * col_moment_ref[...] + 0.1 * (column_sum / D)
    new_cols_ref[...] = new_cols
    update_total = row_mean * jnp.sum(scaled_sum / new_cols, axis=1, keepdims=True)
    new_rows = to_column(rows_ref[...])
    update = grad_ref[...] * lax.rsqrt(new_rows * new_cols / row_mean)
    entries = D * WIDTH
    update_rms = jnp.sqrt(update_total / entries)
    weight_rms = jnp.sqrt(weight_total / entries + 1e-06)
    factor = 0.05 * weight_rms / jnp.maximum(jnp.float32(1.0), update_rms)
    new_weight_ref[...] = weight_ref[...] - factor * update


def apply_update(small, grad, new_rows, weight, col_moment):
    return pl.pallas_call(
        update_kernel,
        in_specs=[HERE] * 5,
        out_specs=(HERE,) * 3,
        out_shape=(
            jax.ShapeDtypeStruct((ROWS, WIDTH), jnp.float32),
            jax.ShapeDtypeStruct((1, ROWS), jnp.float32),
            jax.ShapeDtypeStruct((1, WIDTH), jnp.float32),
        ),
    )(*(in_vmem(array) for array in (small, grad, new_rows, weight, col_moment)))


def copies_of(value, axes, count):
    return lax.all_to_all(jnp.broadcast_to(value[None], (count,) + value.shape), axes, 0, 0, tiled=True)


def body(inputs, out_grad, weight, row_moment, col_moment):
    parts = token_product(inputs, out_grad)
    parts = lax.all_to_all(parts, AXES, 0, 0, tiled=True, axis_index_groups=near_groups())
    parts = jnp.sum(parts, axis=0)
    parts = lax.all_to_all(parts, AXES, 0, 0, tiled=True, axis_index_groups=far_groups())
    grad, row_values, small = statistics(parts, weight, row_moment.reshape(1, ROWS))
    small = jnp.sum(copies_of(small, ("x", "z"), 32), axis=0)
    small = copies_of(small, ("yh", "yl", "c"), 16)
    new_weight, new_rows, new_cols = apply_update(small, grad, row_values, weight, col_moment.reshape(1, WIDTH))
    return (new_weight, new_rows.reshape(ROWS), new_cols.reshape(WIDTH))


def solution(mesh):
    fine = Mesh(mesh.devices.reshape(SIZES), AXES)
    placed = (P(DP, MP), P(DP, None), P(MP + DP, None), P(MP + DP), P())
    return jax.shard_map(
        body,
        mesh=fine,
        in_specs=placed,
        out_specs=(P(MP + DP, None), P(MP + DP), P()),
        check_vma=False,
    )
```

```python
import jax
import jax.numpy as jnp
from jax import lax
from jax.experimental import pallas as pl
from jax.experimental.pallas import tpu as pltpu
from jax.sharding import Mesh, PartitionSpec as P

D = 8192
WIDTH = 512
ROWS = 16
LANES = 128
MIB = 1024 * 1024
AXES = ("yh", "x", "z", "yl", "c")
SIZES = (2, 4, 8, 4, 2)
DP = ("yh", "x", "z")
MP = ("yl", "c")
SMALL = 2 * WIDTH + 2 * LANES
MOMENTS = 2 * ROWS
SQUARES = MOMENTS + 1
CARRIED = 2 * ROWS + 8


CLASS_X = ((1, 2), (0, 3))
CLASS_Z = ((1, 3, 4, 6), (0, 2, 5, 7))
BLOCKS_X = ((0, 1), (2, 3))
BLOCKS_Z = ((0, 1), (2, 3), (4, 5), (6, 7))


def place(yh, x, z, yl, c):
    return (((yh * 4 + (x + c) % 4) * 8 + (z + c) % 8) * 4 + yl) * 2 + c


def near_groups():
    return [
        [
            place(yh, next(x for x in xs if x in class_x), next(z for z in zs if z in class_z), yl, c)
            for class_x in CLASS_X
            for class_z in CLASS_Z
        ]
        for yh in range(2)
        for xs in BLOCKS_X
        for zs in BLOCKS_Z
        for yl in range(4)
        for c in range(2)
    ]


def far_groups():
    return [
        [place(yh, x, z, yl, c) for x in class_x for z in class_z]
        for class_x in CLASS_X
        for class_z in CLASS_Z
        for yh in range(2)
        for yl in range(4)
        for c in range(2)
    ]


def position(yh, x, z, core):
    x, z = (x - core) % 4, (z - core) % 8
    kx = next(k for k, xs in enumerate(CLASS_X) if x in xs)
    kz = next(k for k, zs in enumerate(CLASS_Z) if z in zs)
    return 2 * kx + kz, (CLASS_X[kx].index(x) * 4 + CLASS_Z[kz].index(z)) * 2 + yh


CHUNKS = (512, 512, 640)
BLOCKS = 4
HERE = pl.BlockSpec(memory_space=pltpu.VMEM)


def in_vmem(array):
    return pltpu.with_memory_space_constraint(array, pltpu.VMEM)


def in_hbm(array):
    return pltpu.with_memory_space_constraint(array, pltpu.HBM)


def product_kernel(inputs_ref, columns_ref, out_ref, inputs, columns, total, in_sems, column_sems):
    core = lax.axis_index("c")
    copies = []
    first = 0
    for i, tokens in enumerate(CHUNKS):
        span = pl.ds(first, tokens)
        pair = (
            pltpu.make_async_copy(columns_ref.at[span], columns.at[span], column_sems.at[i]),
            pltpu.make_async_copy(inputs_ref.at[span], inputs.at[span], in_sems.at[i]),
        )
        for copy in pair:
            copy.start()
        copies.append((first, tokens, pair))
        first += tokens
    size = inputs.shape[1] // BLOCKS
    for i, (first, tokens, pair) in enumerate(copies):
        for copy in pair:
            copy.wait()
        for block in range(BLOCKS):
            rows = slice(block * size, (block + 1) * size)
            product = lax.dot_general(
                inputs[first : first + tokens, rows],
                columns[first : first + tokens],
                (((0,), (0,)), ((), ())),
                preferred_element_type=jnp.float32,
            )
            if i > 0:
                product = product + total[rows]
            if i < len(CHUNKS) - 1:
                total[rows] = product
                continue
            for r in range(size // ROWS):
                device = block * (size // ROWS) + r
                where = device // 32, device // 8 % 4, device % 8
                (kind, index), (kind1, index1) = position(*where, 0), position(*where, 1)
                kind, index = kind + core * (kind1 - kind), index + core * (index1 - index)
                out_ref[kind, index] = product[r * ROWS : (r + 1) * ROWS]


def token_product(inputs, out_grad):
    tokens, rows = inputs.shape
    return pl.pallas_call(
        product_kernel,
        in_specs=[pl.BlockSpec(memory_space=pl.ANY)] * 2,
        out_specs=HERE,
        out_shape=pltpu.VMEM((4, 16, ROWS, WIDTH), jnp.float32),
        scratch_shapes=[
            pltpu.VMEM((tokens, rows), jnp.bfloat16),
            pltpu.VMEM((tokens, WIDTH), jnp.bfloat16),
            pltpu.VMEM((rows, WIDTH), jnp.float32),
            pltpu.SemaphoreType.DMA((len(CHUNKS),)),
            pltpu.SemaphoreType.DMA((len(CHUNKS),)),
        ],
        compiler_params=pltpu.CompilerParams(vmem_limit_bytes=24 * MIB),
    )(in_hbm(inputs), in_hbm(out_grad))


def diagonal():
    return lax.broadcasted_iota(jnp.int32, (ROWS, ROWS), 0) == lax.broadcasted_iota(jnp.int32, (ROWS, ROWS), 1)


def to_column(row):
    return jnp.sum(jnp.where(diagonal(), row, 0.0), axis=1, keepdims=True)


def to_row(column):
    return jnp.sum(jnp.where(diagonal(), column, 0.0), axis=0, keepdims=True)


def pack_kernel(parts_ref, weight_ref, row_moment_ref, out_ref):
    total = jnp.sum(parts_ref[...], axis=0)
    for half in range(2):
        out_ref[half * ROWS : (half + 1) * ROWS] = total[half]
    out_ref[MOMENTS:] = jnp.zeros((CARRIED - MOMENTS, WIDTH), jnp.float32)
    out_ref[MOMENTS : MOMENTS + 1, :ROWS] = row_moment_ref[...]
    out_ref[SQUARES : SQUARES + 1] = jnp.sum(weight_ref[...] * weight_ref[...], axis=0, keepdims=True)


def pack(parts, weight, row_moment):
    return pl.pallas_call(
        pack_kernel,
        in_specs=[HERE] * 3,
        out_specs=HERE,
        out_shape=pltpu.VMEM((CARRIED, WIDTH), jnp.float32),
    )(in_vmem(parts), in_vmem(weight), in_vmem(row_moment))


def statistics_kernel(mine_ref, other_ref, grad_ref, rows_ref, small_ref):
    half = lax.axis_index("yh")

    def rows_of(which, moments_ref):
        span = pl.ds(pl.multiple_of(which * ROWS, ROWS), ROWS)
        grad = mine_ref[span, :] + other_ref[span, :]
        squares = grad * grad
        moments = to_column(moments_ref[MOMENTS : MOMENTS + 1, :ROWS])
        new_rows = 0.9 * moments + 0.1 * (jnp.sum(squares, axis=1, keepdims=True) / WIDTH)
        plain = jnp.sum(squares, axis=0, keepdims=True)
        scaled = jnp.sum(squares / new_rows, axis=0, keepdims=True)
        return grad, to_row(new_rows), plain, scaled

    grad, new_rows, plain, scaled = rows_of(half, mine_ref)
    _, far_rows, far_plain, far_scaled = rows_of(1 - half, other_ref)
    grad_ref[...] = grad
    rows_ref[...] = new_rows
    weight_squares = mine_ref[SQUARES : SQUARES + 1] + other_ref[SQUARES : SQUARES + 1]
    small_ref[:, :WIDTH] = plain + far_plain
    small_ref[:, WIDTH : 2 * WIDTH] = scaled + far_scaled
    small_ref[:, 2 * WIDTH : 2 * WIDTH + LANES] = sum(
        weight_squares[:, i : i + LANES] for i in range(0, WIDTH, LANES)
    )
    small_ref[:, 2 * WIDTH + LANES :] = jnp.zeros((1, LANES), jnp.float32)
    small_ref[:, 2 * WIDTH + LANES : 2 * WIDTH + LANES + ROWS] = new_rows + far_rows


def statistics(mine, other):
    return pl.pallas_call(
        statistics_kernel,
        in_specs=[HERE] * 2,
        out_specs=(HERE,) * 3,
        out_shape=(
            pltpu.VMEM((ROWS, WIDTH), jnp.float32),
            pltpu.VMEM((1, ROWS), jnp.float32),
            pltpu.VMEM((1, SMALL), jnp.float32),
        ),
    )(in_vmem(mine), in_vmem(other))


def update_kernel(small_ref, grad_ref, rows_ref, weight_ref, col_moment_ref, new_weight_ref, new_rows_ref, new_cols_ref):
    new_rows_ref[...] = rows_ref[...]
    small = jnp.sum(small_ref[...], axis=0)
    column_sum, scaled_sum = small[:, :WIDTH], small[:, WIDTH : 2 * WIDTH]
    weight_total = jnp.sum(small[:, 2 * WIDTH : 2 * WIDTH + LANES], axis=1, keepdims=True)
    row_mean = jnp.sum(small[:, 2 * WIDTH + LANES :], axis=1, keepdims=True) / D
    new_cols = 0.9 * col_moment_ref[...] + 0.1 * (column_sum / D)
    new_cols_ref[...] = new_cols
    update_total = row_mean * jnp.sum(scaled_sum / new_cols, axis=1, keepdims=True)
    new_rows = to_column(rows_ref[...])
    update = grad_ref[...] * lax.rsqrt(new_rows * new_cols / row_mean)
    entries = D * WIDTH
    update_rms = jnp.sqrt(update_total / entries)
    weight_rms = jnp.sqrt(weight_total / entries + 1e-06)
    factor = 0.05 * weight_rms / jnp.maximum(jnp.float32(1.0), update_rms)
    new_weight_ref[...] = weight_ref[...] - factor * update


def apply_update(small, grad, new_rows, weight, col_moment):
    return pl.pallas_call(
        update_kernel,
        in_specs=[HERE] * 5,
        out_specs=(HERE,) * 3,
        out_shape=(
            jax.ShapeDtypeStruct((ROWS, WIDTH), jnp.float32),
            jax.ShapeDtypeStruct((1, ROWS), jnp.float32),
            jax.ShapeDtypeStruct((1, WIDTH), jnp.float32),
        ),
    )(*(in_vmem(array) for array in (small, grad, new_rows, weight, col_moment)))


def copies_of(value, axes, count):
    return lax.all_to_all(jnp.broadcast_to(value[None], (count,) + value.shape), axes, 0, 0, tiled=True)


def body(inputs, out_grad, weight, row_moment, col_moment):
    parts = token_product(inputs, out_grad)
    parts = lax.all_to_all(parts, AXES, 0, 0, tiled=True, axis_index_groups=near_groups())
    parts = jnp.sum(parts, axis=0).reshape(8, 2, ROWS, WIDTH)
    parts = lax.all_to_all(parts, AXES, 0, 0, tiled=True, axis_index_groups=far_groups())
    mine = pack(parts, weight, row_moment.reshape(1, ROWS))
    other = lax.ppermute(mine, "yh", [(0, 1), (1, 0)])
    grad, row_values, small = statistics(mine, other)
    small = jnp.sum(copies_of(small, ("x", "z"), 32), axis=0)
    small = copies_of(small, ("yl", "c"), 8)
    new_weight, new_rows, new_cols = apply_update(small, grad, row_values, weight, col_moment.reshape(1, WIDTH))
    return (new_weight, new_rows.reshape(ROWS), new_cols.reshape(WIDTH))


def solution(mesh):
    fine = Mesh(mesh.devices.reshape(SIZES), AXES)
    placed = (P(DP, MP), P(DP, None), P(MP + DP, None), P(MP + DP), P())
    return jax.shard_map(
        body,
        mesh=fine,
        in_specs=placed,
        out_specs=(P(MP + DP, None), P(MP + DP), P()),
        check_vma=False,
    )
```

```python
import jax
import jax.numpy as jnp
from jax import lax
from jax.experimental import pallas as pl
from jax.experimental.pallas import tpu as pltpu
from jax.sharding import Mesh, PartitionSpec as P

D = 8192
WIDTH = 512
ROWS = 16
LANES = 128
MIB = 1024 * 1024
AXES = ("yh", "x", "z", "yl", "c")
SIZES = (2, 4, 8, 4, 2)
DP = ("yh", "x", "z")
MP = ("yl", "c")
SMALL = 2 * WIDTH + 2 * LANES
MOMENTS = 2 * ROWS
SQUARES = MOMENTS + 1
CARRIED = 2 * ROWS + 8


CLASS_X = ((1, 2), (0, 3))
CLASS_Z = ((1, 3, 4, 6), (0, 2, 5, 7))
BLOCKS_X = ((0, 1), (2, 3))
BLOCKS_Z = ((0, 1), (2, 3), (4, 5), (6, 7))


def place(yh, x, z, yl, c):
    return (((yh * 4 + (x + c) % 4) * 8 + (z + c) % 8) * 4 + yl) * 2 + c


def near_groups():
    return [
        [
            place(yh, next(x for x in xs if x in class_x), next(z for z in zs if z in class_z), yl, c)
            for class_x in CLASS_X
            for class_z in CLASS_Z
        ]
        for yh in range(2)
        for xs in BLOCKS_X
        for zs in BLOCKS_Z
        for yl in range(4)
        for c in range(2)
    ]


def far_groups():
    return [
        [place(yh, x, z, yl, c) for x in class_x for z in class_z]
        for class_x in CLASS_X
        for class_z in CLASS_Z
        for yh in range(2)
        for yl in range(4)
        for c in range(2)
    ]


def position(yh, x, z, core):
    x, z = (x - core) % 4, (z - core) % 8
    kx = next(k for k, xs in enumerate(CLASS_X) if x in xs)
    kz = next(k for k, zs in enumerate(CLASS_Z) if z in zs)
    return 2 * kx + kz, (CLASS_X[kx].index(x) * 4 + CLASS_Z[kz].index(z)) * 2 + yh


CHUNKS = (512, 512, 640)
BLOCKS = 4
HERE = pl.BlockSpec(memory_space=pltpu.VMEM)


def in_vmem(array):
    return pltpu.with_memory_space_constraint(array, pltpu.VMEM)


def in_hbm(array):
    return pltpu.with_memory_space_constraint(array, pltpu.HBM)


def product_kernel(inputs_ref, columns_ref, out_ref, inputs, columns, total, in_sems, column_sems):
    core = lax.axis_index("c")
    copies = []
    first = 0
    for i, tokens in enumerate(CHUNKS):
        span = pl.ds(first, tokens)
        pair = (
            pltpu.make_async_copy(columns_ref.at[span], columns.at[span], column_sems.at[i]),
            pltpu.make_async_copy(inputs_ref.at[span], inputs.at[span], in_sems.at[i]),
        )
        for copy in pair:
            copy.start()
        copies.append((first, tokens, pair))
        first += tokens
    size = inputs.shape[1] // BLOCKS
    for i, (first, tokens, pair) in enumerate(copies):
        for copy in pair:
            copy.wait()
        for block in range(BLOCKS):
            rows = slice(block * size, (block + 1) * size)
            product = lax.dot_general(
                inputs[first : first + tokens, rows],
                columns[first : first + tokens],
                (((0,), (0,)), ((), ())),
                preferred_element_type=jnp.float32,
            )
            if i > 0:
                product = product + total[rows]
            if i < len(CHUNKS) - 1:
                total[rows] = product
                continue
            for r in range(size // ROWS):
                device = block * (size // ROWS) + r
                where = device // 32, device // 8 % 4, device % 8
                (kind, index), (kind1, index1) = position(*where, 0), position(*where, 1)
                kind, index = kind + core * (kind1 - kind), index + core * (index1 - index)
                out_ref[kind, index] = product[r * ROWS : (r + 1) * ROWS]


def token_product(inputs, out_grad):
    tokens, rows = inputs.shape
    return pl.pallas_call(
        product_kernel,
        in_specs=[pl.BlockSpec(memory_space=pl.ANY)] * 2,
        out_specs=HERE,
        out_shape=pltpu.VMEM((4, 16, ROWS, WIDTH), jnp.float32),
        scratch_shapes=[
            pltpu.VMEM((tokens, rows), jnp.bfloat16),
            pltpu.VMEM((tokens, WIDTH), jnp.bfloat16),
            pltpu.VMEM((rows, WIDTH), jnp.float32),
            pltpu.SemaphoreType.DMA((len(CHUNKS),)),
            pltpu.SemaphoreType.DMA((len(CHUNKS),)),
        ],
        compiler_params=pltpu.CompilerParams(vmem_limit_bytes=24 * MIB),
    )(in_hbm(inputs), in_hbm(out_grad))


def diagonal():
    return lax.broadcasted_iota(jnp.int32, (ROWS, ROWS), 0) == lax.broadcasted_iota(jnp.int32, (ROWS, ROWS), 1)


def to_column(row):
    return jnp.sum(jnp.where(diagonal(), row, 0.0), axis=1, keepdims=True)


def to_row(column):
    return jnp.sum(jnp.where(diagonal(), column, 0.0), axis=0, keepdims=True)


def pack_kernel(parts_ref, weight_ref, row_moment_ref, out_ref):
    total = jnp.sum(parts_ref[...], axis=0)
    for half in range(2):
        out_ref[half * ROWS : (half + 1) * ROWS] = total[half]
    out_ref[MOMENTS:] = jnp.zeros((CARRIED - MOMENTS, WIDTH), jnp.float32)
    out_ref[MOMENTS : MOMENTS + 1, :ROWS] = row_moment_ref[...]
    out_ref[SQUARES : SQUARES + 1] = jnp.sum(weight_ref[...] * weight_ref[...], axis=0, keepdims=True)


def pack(parts, weight, row_moment):
    return pl.pallas_call(
        pack_kernel,
        in_specs=[HERE] * 3,
        out_specs=HERE,
        out_shape=pltpu.VMEM((CARRIED, WIDTH), jnp.float32),
    )(in_vmem(parts), in_vmem(weight), in_vmem(row_moment))


def statistics_kernel(mine_ref, other_ref, grad_ref, rows_ref, small_ref):
    half = lax.axis_index("yh")

    def rows_of(which, moments_ref):
        span = pl.ds(pl.multiple_of(which * ROWS, ROWS), ROWS)
        grad = mine_ref[span, :] + other_ref[span, :]
        squares = grad * grad
        moments = to_column(moments_ref[MOMENTS : MOMENTS + 1, :ROWS])
        new_rows = 0.9 * moments + 0.1 * (jnp.sum(squares, axis=1, keepdims=True) / WIDTH)
        plain = jnp.sum(squares, axis=0, keepdims=True)
        scaled = jnp.sum(squares / new_rows, axis=0, keepdims=True)
        return grad, to_row(new_rows), plain, scaled

    grad, new_rows, plain, scaled = rows_of(half, mine_ref)
    _, far_rows, far_plain, far_scaled = rows_of(1 - half, other_ref)
    grad_ref[...] = grad
    rows_ref[...] = new_rows
    weight_squares = mine_ref[SQUARES : SQUARES + 1] + other_ref[SQUARES : SQUARES + 1]
    small_ref[:, :WIDTH] = plain + far_plain
    small_ref[:, WIDTH : 2 * WIDTH] = scaled + far_scaled
    small_ref[:, 2 * WIDTH : 2 * WIDTH + LANES] = sum(
        weight_squares[:, i : i + LANES] for i in range(0, WIDTH, LANES)
    )
    small_ref[:, 2 * WIDTH + LANES :] = jnp.zeros((1, LANES), jnp.float32)
    small_ref[:, 2 * WIDTH + LANES : 2 * WIDTH + LANES + ROWS] = new_rows + far_rows


def statistics(mine, other):
    return pl.pallas_call(
        statistics_kernel,
        in_specs=[HERE] * 2,
        out_specs=(HERE,) * 3,
        out_shape=(
            pltpu.VMEM((ROWS, WIDTH), jnp.float32),
            pltpu.VMEM((1, ROWS), jnp.float32),
            pltpu.VMEM((1, SMALL), jnp.float32),
        ),
    )(in_vmem(mine), in_vmem(other))


def update_kernel(small_ref, grad_ref, rows_ref, weight_ref, col_moment_ref, new_weight_ref, new_rows_ref, new_cols_ref):
    new_rows_ref[...] = rows_ref[...]
    small = jnp.sum(small_ref[...], axis=0)
    column_sum, scaled_sum = small[:, :WIDTH], small[:, WIDTH : 2 * WIDTH]
    weight_total = jnp.sum(small[:, 2 * WIDTH : 2 * WIDTH + LANES], axis=1, keepdims=True)
    row_mean = jnp.sum(small[:, 2 * WIDTH + LANES :], axis=1, keepdims=True) / D
    new_cols = 0.9 * col_moment_ref[...] + 0.1 * (column_sum / D)
    new_cols_ref[...] = new_cols
    update_total = row_mean * jnp.sum(scaled_sum / new_cols, axis=1, keepdims=True)
    new_rows = to_column(rows_ref[...])
    update = grad_ref[...] * lax.rsqrt(new_rows * new_cols / row_mean)
    entries = D * WIDTH
    update_rms = jnp.sqrt(update_total / entries)
    weight_rms = jnp.sqrt(weight_total / entries + 1e-06)
    factor = 0.05 * weight_rms / jnp.maximum(jnp.float32(1.0), update_rms)
    new_weight_ref[...] = weight_ref[...] - factor * update


def apply_update(small, grad, new_rows, weight, col_moment):
    return pl.pallas_call(
        update_kernel,
        in_specs=[HERE] * 5,
        out_specs=(HERE,) * 3,
        out_shape=(
            jax.ShapeDtypeStruct((ROWS, WIDTH), jnp.float32),
            jax.ShapeDtypeStruct((1, ROWS), jnp.float32),
            jax.ShapeDtypeStruct((1, WIDTH), jnp.float32),
        ),
    )(*(in_vmem(array) for array in (small, grad, new_rows, weight, col_moment)))


def copies_of(value, axes, count):
    return lax.all_to_all(jnp.broadcast_to(value[None], (count,) + value.shape), axes, 0, 0, tiled=True)


def body(inputs, out_grad, weight, row_moment, col_moment):
    parts = token_product(inputs, out_grad)
    parts = lax.all_to_all(parts, AXES, 0, 0, tiled=True, axis_index_groups=near_groups())
    parts = jnp.sum(parts, axis=0).reshape(8, 2, ROWS, WIDTH)
    parts = lax.all_to_all(parts, AXES, 0, 0, tiled=True, axis_index_groups=far_groups())
    mine = pack(parts, weight, row_moment.reshape(1, ROWS))
    other = lax.ppermute(mine, "yh", [(0, 1), (1, 0)])
    grad, row_values, small = statistics(mine, other)
    small = jnp.sum(copies_of(small, ("yl", "c"), 8), axis=0)
    small = copies_of(small, ("x", "z"), 32)
    new_weight, new_rows, new_cols = apply_update(small, grad, row_values, weight, col_moment.reshape(1, WIDTH))
    return (new_weight, new_rows.reshape(ROWS), new_cols.reshape(WIDTH))


def solution(mesh):
    fine = Mesh(mesh.devices.reshape(SIZES), AXES)
    placed = (P(DP, MP), P(DP, None), P(MP + DP, None), P(MP + DP), P())
    return jax.shard_map(
        body,
        mesh=fine,
        in_specs=placed,
        out_specs=(P(MP + DP, None), P(MP + DP), P()),
        check_vma=False,
    )
```

```python
import jax
import jax.numpy as jnp
from jax import lax
from jax.experimental import pallas as pl
from jax.experimental.pallas import tpu as pltpu
from jax.sharding import Mesh, PartitionSpec as P

D = 8192
WIDTH = 512
ROWS = 16
LANES = 128
MIB = 1024 * 1024
AXES = ("yh", "x", "z", "yl", "c")
SIZES = (2, 4, 8, 4, 2)
DP = ("yh", "x", "z")
MP = ("yl", "c")
SMALL = 2 * WIDTH + LANES
HALF = LANES // 2
MOMENTS = 2 * ROWS
SQUARES = MOMENTS + 1
CARRIED = 2 * ROWS + 8


CLASS_X = ((1, 2), (0, 3))
CLASS_Z = ((1, 3, 4, 6), (0, 2, 5, 7))
BLOCKS_X = ((0, 1), (2, 3))
BLOCKS_Z = ((0, 1), (2, 3), (4, 5), (6, 7))


def place(yh, x, z, yl, c):
    return (((yh * 4 + (x + c) % 4) * 8 + (z + c) % 8) * 4 + yl) * 2 + c


def near_groups():
    return [
        [
            place(yh, next(x for x in xs if x in class_x), next(z for z in zs if z in class_z), yl, c)
            for class_x in CLASS_X
            for class_z in CLASS_Z
        ]
        for yh in range(2)
        for xs in BLOCKS_X
        for zs in BLOCKS_Z
        for yl in range(4)
        for c in range(2)
    ]


def far_groups():
    return [
        [place(yh, x, z, yl, c) for x in class_x for z in class_z]
        for class_x in CLASS_X
        for class_z in CLASS_Z
        for yh in range(2)
        for yl in range(4)
        for c in range(2)
    ]


def position(yh, x, z, core):
    x, z = (x - core) % 4, (z - core) % 8
    kx = next(k for k, xs in enumerate(CLASS_X) if x in xs)
    kz = next(k for k, zs in enumerate(CLASS_Z) if z in zs)
    return 2 * kx + kz, (CLASS_X[kx].index(x) * 4 + CLASS_Z[kz].index(z)) * 2 + yh


CHUNKS = (512, 512, 640)
BLOCKS = 4
HERE = pl.BlockSpec(memory_space=pltpu.VMEM)


def in_vmem(array):
    return pltpu.with_memory_space_constraint(array, pltpu.VMEM)


def in_hbm(array):
    return pltpu.with_memory_space_constraint(array, pltpu.HBM)


def product_kernel(inputs_ref, columns_ref, out_ref, inputs, columns, total, in_sems, column_sems):
    core = lax.axis_index("c")
    copies = []
    first = 0
    for i, tokens in enumerate(CHUNKS):
        span = pl.ds(first, tokens)
        pair = (
            pltpu.make_async_copy(columns_ref.at[span], columns.at[span], column_sems.at[i]),
            pltpu.make_async_copy(inputs_ref.at[span], inputs.at[span], in_sems.at[i]),
        )
        for copy in pair:
            copy.start()
        copies.append((first, tokens, pair))
        first += tokens
    size = inputs.shape[1] // BLOCKS
    for i, (first, tokens, pair) in enumerate(copies):
        for copy in pair:
            copy.wait()
        for block in range(BLOCKS):
            rows = slice(block * size, (block + 1) * size)
            product = lax.dot_general(
                inputs[first : first + tokens, rows],
                columns[first : first + tokens],
                (((0,), (0,)), ((), ())),
                preferred_element_type=jnp.float32,
            )
            if i > 0:
                product = product + total[rows]
            if i < len(CHUNKS) - 1:
                total[rows] = product
                continue
            for r in range(size // ROWS):
                device = block * (size // ROWS) + r
                where = device // 32, device // 8 % 4, device % 8
                (kind, index), (kind1, index1) = position(*where, 0), position(*where, 1)
                kind, index = kind + core * (kind1 - kind), index + core * (index1 - index)
                out_ref[kind, index] = product[r * ROWS : (r + 1) * ROWS]


def token_product(inputs, out_grad):
    tokens, rows = inputs.shape
    return pl.pallas_call(
        product_kernel,
        in_specs=[pl.BlockSpec(memory_space=pl.ANY)] * 2,
        out_specs=HERE,
        out_shape=pltpu.VMEM((4, 16, ROWS, WIDTH), jnp.float32),
        scratch_shapes=[
            pltpu.VMEM((tokens, rows), jnp.bfloat16),
            pltpu.VMEM((tokens, WIDTH), jnp.bfloat16),
            pltpu.VMEM((rows, WIDTH), jnp.float32),
            pltpu.SemaphoreType.DMA((len(CHUNKS),)),
            pltpu.SemaphoreType.DMA((len(CHUNKS),)),
        ],
        compiler_params=pltpu.CompilerParams(vmem_limit_bytes=24 * MIB),
    )(in_hbm(inputs), in_hbm(out_grad))


def diagonal():
    return lax.broadcasted_iota(jnp.int32, (ROWS, ROWS), 0) == lax.broadcasted_iota(jnp.int32, (ROWS, ROWS), 1)


def to_column(row):
    return jnp.sum(jnp.where(diagonal(), row, 0.0), axis=1, keepdims=True)


def to_row(column):
    return jnp.sum(jnp.where(diagonal(), column, 0.0), axis=0, keepdims=True)


def pack_kernel(parts_ref, weight_ref, row_moment_ref, out_ref):
    total = jnp.sum(parts_ref[...], axis=0)
    for half in range(2):
        out_ref[half * ROWS : (half + 1) * ROWS] = total[half]
    out_ref[MOMENTS:] = jnp.zeros((CARRIED - MOMENTS, WIDTH), jnp.float32)
    out_ref[MOMENTS : MOMENTS + 1, :ROWS] = row_moment_ref[...]
    out_ref[SQUARES : SQUARES + 1] = jnp.sum(weight_ref[...] * weight_ref[...], axis=0, keepdims=True)


def pack(parts, weight, row_moment):
    return pl.pallas_call(
        pack_kernel,
        in_specs=[HERE] * 3,
        out_specs=HERE,
        out_shape=pltpu.VMEM((CARRIED, WIDTH), jnp.float32),
    )(in_vmem(parts), in_vmem(weight), in_vmem(row_moment))


def statistics_kernel(mine_ref, other_ref, grad_ref, rows_ref, small_ref):
    half = lax.axis_index("yh")

    def rows_of(which, moments_ref):
        span = pl.ds(pl.multiple_of(which * ROWS, ROWS), ROWS)
        grad = mine_ref[span, :] + other_ref[span, :]
        squares = grad * grad
        moments = to_column(moments_ref[MOMENTS : MOMENTS + 1, :ROWS])
        new_rows = 0.9 * moments + 0.1 * (jnp.sum(squares, axis=1, keepdims=True) / WIDTH)
        plain = jnp.sum(squares, axis=0, keepdims=True)
        scaled = jnp.sum(squares / new_rows, axis=0, keepdims=True)
        return grad, to_row(new_rows), plain, scaled

    grad, new_rows, plain, scaled = rows_of(half, mine_ref)
    _, far_rows, far_plain, far_scaled = rows_of(1 - half, other_ref)
    grad_ref[...] = grad
    rows_ref[...] = new_rows
    weight_squares = mine_ref[SQUARES : SQUARES + 1] + other_ref[SQUARES : SQUARES + 1]
    small_ref[:, :WIDTH] = plain + far_plain
    small_ref[:, WIDTH : 2 * WIDTH] = scaled + far_scaled
    small_ref[:, 2 * WIDTH :] = jnp.zeros((1, LANES), jnp.float32)
    small_ref[:, 2 * WIDTH : 2 * WIDTH + HALF] = sum(weight_squares[:, i : i + HALF] for i in range(0, WIDTH, HALF))
    small_ref[:, 2 * WIDTH + HALF : 2 * WIDTH + HALF + ROWS] = new_rows + far_rows


def statistics(mine, other):
    return pl.pallas_call(
        statistics_kernel,
        in_specs=[HERE] * 2,
        out_specs=(HERE,) * 3,
        out_shape=(
            pltpu.VMEM((ROWS, WIDTH), jnp.float32),
            pltpu.VMEM((1, ROWS), jnp.float32),
            pltpu.VMEM((1, SMALL), jnp.float32),
        ),
    )(in_vmem(mine), in_vmem(other))


def update_kernel(small_ref, grad_ref, rows_ref, weight_ref, col_moment_ref, new_weight_ref, new_rows_ref, new_cols_ref):
    new_rows_ref[...] = rows_ref[...]
    small = jnp.sum(small_ref[...], axis=0)
    column_sum, scaled_sum = small[:, :WIDTH], small[:, WIDTH : 2 * WIDTH]
    weight_total = jnp.sum(small[:, 2 * WIDTH : 2 * WIDTH + HALF], axis=1, keepdims=True)
    row_mean = jnp.sum(small[:, 2 * WIDTH + HALF :], axis=1, keepdims=True) / D
    new_cols = 0.9 * col_moment_ref[...] + 0.1 * (column_sum / D)
    new_cols_ref[...] = new_cols
    update_total = row_mean * jnp.sum(scaled_sum / new_cols, axis=1, keepdims=True)
    new_rows = to_column(rows_ref[...])
    update = grad_ref[...] * lax.rsqrt(new_rows * new_cols / row_mean)
    entries = D * WIDTH
    update_rms = jnp.sqrt(update_total / entries)
    weight_rms = jnp.sqrt(weight_total / entries + 1e-06)
    factor = 0.05 * weight_rms / jnp.maximum(jnp.float32(1.0), update_rms)
    new_weight_ref[...] = weight_ref[...] - factor * update


def apply_update(small, grad, new_rows, weight, col_moment):
    return pl.pallas_call(
        update_kernel,
        in_specs=[HERE] * 5,
        out_specs=(HERE,) * 3,
        out_shape=(
            jax.ShapeDtypeStruct((ROWS, WIDTH), jnp.float32),
            jax.ShapeDtypeStruct((1, ROWS), jnp.float32),
            jax.ShapeDtypeStruct((1, WIDTH), jnp.float32),
        ),
    )(*(in_vmem(array) for array in (small, grad, new_rows, weight, col_moment)))


def copies_of(value, axes, count):
    return lax.all_to_all(jnp.broadcast_to(value[None], (count,) + value.shape), axes, 0, 0, tiled=True)


def body(inputs, out_grad, weight, row_moment, col_moment):
    parts = token_product(inputs, out_grad)
    parts = lax.all_to_all(parts, AXES, 0, 0, tiled=True, axis_index_groups=near_groups())
    parts = jnp.sum(parts, axis=0).reshape(8, 2, ROWS, WIDTH)
    parts = lax.all_to_all(parts, AXES, 0, 0, tiled=True, axis_index_groups=far_groups())
    mine = pack(parts, weight, row_moment.reshape(1, ROWS))
    other = lax.ppermute(mine, "yh", [(0, 1), (1, 0)])
    grad, row_values, small = statistics(mine, other)
    small = jnp.sum(copies_of(small, ("yl", "c"), 8), axis=0)
    small = copies_of(small, ("x", "z"), 32)
    new_weight, new_rows, new_cols = apply_update(small, grad, row_values, weight, col_moment.reshape(1, WIDTH))
    return (new_weight, new_rows.reshape(ROWS), new_cols.reshape(WIDTH))


def solution(mesh):
    fine = Mesh(mesh.devices.reshape(SIZES), AXES)
    placed = (P(DP, MP), P(DP, None), P(MP + DP, None), P(MP + DP), P())
    return jax.shard_map(
        body,
        mesh=fine,
        in_specs=placed,
        out_specs=(P(MP + DP, None), P(MP + DP), P()),
        check_vma=False,
    )
```

```python
import jax
import jax.numpy as jnp
from jax import lax
from jax.experimental import pallas as pl
from jax.experimental.pallas import tpu as pltpu
from jax.sharding import Mesh, PartitionSpec as P

D = 8192
WIDTH = 512
ROWS = 16
LANES = 128
MIB = 1024 * 1024
AXES = ("yh", "x", "z", "yl", "c")
SIZES = (2, 4, 8, 4, 2)
DP = ("yh", "x", "z")
MP = ("yl", "c")
SMALL = 2 * WIDTH + LANES
HALF = LANES // 2
MOMENTS = 2 * ROWS
SQUARES = MOMENTS + 1
CARRIED = 2 * ROWS + 8


CLASS_X = ((1, 2), (0, 3))
CLASS_Z = ((1, 3, 4, 6), (0, 2, 5, 7))
BLOCKS_X = ((0, 1), (2, 3))
BLOCKS_Z = ((0, 1), (2, 3), (4, 5), (6, 7))


def place(yh, x, z, yl, c):
    return (((yh * 4 + (x + c) % 4) * 8 + (z + c) % 8) * 4 + yl) * 2 + c


def near_groups():
    return [
        [
            place(yh, next(x for x in xs if x in class_x), next(z for z in zs if z in class_z), yl, c)
            for class_x in CLASS_X
            for class_z in CLASS_Z
        ]
        for yh in range(2)
        for xs in BLOCKS_X
        for zs in BLOCKS_Z
        for yl in range(4)
        for c in range(2)
    ]


def far_groups():
    return [
        [place(yh, x, z, yl, c) for x in class_x for z in class_z]
        for class_x in CLASS_X
        for class_z in CLASS_Z
        for yh in range(2)
        for yl in range(4)
        for c in range(2)
    ]


def position(yh, x, z, core):
    x, z = (x - core) % 4, (z - core) % 8
    kx = next(k for k, xs in enumerate(CLASS_X) if x in xs)
    kz = next(k for k, zs in enumerate(CLASS_Z) if z in zs)
    return 2 * kx + kz, (CLASS_X[kx].index(x) * 4 + CLASS_Z[kz].index(z)) * 2 + yh


CHUNKS = (512, 512, 640)
BLOCKS = 4
HERE = pl.BlockSpec(memory_space=pltpu.VMEM)


def in_vmem(array):
    return pltpu.with_memory_space_constraint(array, pltpu.VMEM)


def in_hbm(array):
    return pltpu.with_memory_space_constraint(array, pltpu.HBM)


def product_kernel(inputs_ref, columns_ref, out_ref, inputs, columns, total, in_sems, column_sems):
    core = lax.axis_index("c")
    copies = []
    first = 0
    for i, tokens in enumerate(CHUNKS):
        span = pl.ds(first, tokens)
        pair = (
            pltpu.make_async_copy(columns_ref.at[span], columns.at[span], column_sems.at[i]),
            pltpu.make_async_copy(inputs_ref.at[span], inputs.at[span], in_sems.at[i]),
        )
        for copy in pair:
            copy.start()
        copies.append((first, tokens, pair))
        first += tokens
    size = inputs.shape[1] // BLOCKS
    for i, (first, tokens, pair) in enumerate(copies):
        for copy in pair:
            copy.wait()
        for block in range(BLOCKS):
            rows = slice(block * size, (block + 1) * size)
            product = lax.dot_general(
                inputs[first : first + tokens, rows],
                columns[first : first + tokens],
                (((0,), (0,)), ((), ())),
                preferred_element_type=jnp.float32,
            )
            if i > 0:
                product = product + total[rows]
            if i < len(CHUNKS) - 1:
                total[rows] = product
                continue
            for r in range(size // ROWS):
                device = block * (size // ROWS) + r
                where = device // 32, device // 8 % 4, device % 8
                (kind, index), (kind1, index1) = position(*where, 0), position(*where, 1)
                kind, index = kind + core * (kind1 - kind), index + core * (index1 - index)
                out_ref[kind, index] = product[r * ROWS : (r + 1) * ROWS]


def token_product(inputs, out_grad):
    tokens, rows = inputs.shape
    return pl.pallas_call(
        product_kernel,
        in_specs=[pl.BlockSpec(memory_space=pl.ANY)] * 2,
        out_specs=HERE,
        out_shape=pltpu.VMEM((4, 16, ROWS, WIDTH), jnp.float32),
        scratch_shapes=[
            pltpu.VMEM((tokens, rows), jnp.bfloat16),
            pltpu.VMEM((tokens, WIDTH), jnp.bfloat16),
            pltpu.VMEM((rows, WIDTH), jnp.float32),
            pltpu.SemaphoreType.DMA((len(CHUNKS),)),
            pltpu.SemaphoreType.DMA((len(CHUNKS),)),
        ],
        compiler_params=pltpu.CompilerParams(vmem_limit_bytes=24 * MIB),
    )(in_hbm(inputs), in_hbm(out_grad))


def diagonal():
    return lax.broadcasted_iota(jnp.int32, (ROWS, ROWS), 0) == lax.broadcasted_iota(jnp.int32, (ROWS, ROWS), 1)


def to_column(row):
    return jnp.sum(jnp.where(diagonal(), row, 0.0), axis=1, keepdims=True)


def to_row(column):
    return jnp.sum(jnp.where(diagonal(), column, 0.0), axis=0, keepdims=True)


def pack_kernel(parts_ref, weight_ref, row_moment_ref, out_ref):
    total = jnp.sum(parts_ref[...], axis=0)
    for half in range(2):
        out_ref[half * ROWS : (half + 1) * ROWS] = total[half]
    out_ref[MOMENTS:] = jnp.zeros((CARRIED - MOMENTS, WIDTH), jnp.float32)
    out_ref[MOMENTS : MOMENTS + 1, :ROWS] = row_moment_ref[...]
    out_ref[SQUARES : SQUARES + 1] = jnp.sum(weight_ref[...] * weight_ref[...], axis=0, keepdims=True)


def pack(parts, weight, row_moment):
    return pl.pallas_call(
        pack_kernel,
        in_specs=[HERE] * 3,
        out_specs=HERE,
        out_shape=pltpu.VMEM((CARRIED, WIDTH), jnp.float32),
    )(in_vmem(parts), in_vmem(weight), in_vmem(row_moment))


def statistics_kernel(mine_ref, other_ref, grad_ref, rows_ref, small_ref):
    half = lax.axis_index("yh")

    def rows_of(which, moments_ref):
        span = pl.ds(pl.multiple_of(which * ROWS, ROWS), ROWS)
        grad = mine_ref[span, :] + other_ref[span, :]
        squares = grad * grad
        moments = to_column(moments_ref[MOMENTS : MOMENTS + 1, :ROWS])
        new_rows = 0.9 * moments + 0.1 * (jnp.sum(squares, axis=1, keepdims=True) / WIDTH)
        plain = jnp.sum(squares, axis=0, keepdims=True)
        scaled = jnp.sum(squares / new_rows, axis=0, keepdims=True)
        return grad, to_row(new_rows), plain, scaled

    grad, new_rows, plain, scaled = rows_of(half, mine_ref)
    _, far_rows, far_plain, far_scaled = rows_of(1 - half, other_ref)
    grad_ref[...] = grad
    rows_ref[...] = new_rows
    weight_squares = mine_ref[SQUARES : SQUARES + 1] + other_ref[SQUARES : SQUARES + 1]
    small_ref[:, :WIDTH] = plain + far_plain
    small_ref[:, WIDTH : 2 * WIDTH] = scaled + far_scaled
    small_ref[:, 2 * WIDTH :] = jnp.zeros((1, LANES), jnp.float32)
    small_ref[:, 2 * WIDTH : 2 * WIDTH + HALF] = sum(weight_squares[:, i : i + HALF] for i in range(0, WIDTH, HALF))
    small_ref[:, 2 * WIDTH + HALF : 2 * WIDTH + HALF + ROWS] = new_rows + far_rows


def statistics(mine, other):
    return pl.pallas_call(
        statistics_kernel,
        in_specs=[HERE] * 2,
        out_specs=(HERE,) * 3,
        out_shape=(
            pltpu.VMEM((ROWS, WIDTH), jnp.float32),
            pltpu.VMEM((1, ROWS), jnp.float32),
            pltpu.VMEM((1, SMALL), jnp.float32),
        ),
    )(in_vmem(mine), in_vmem(other))


def update_kernel(small_ref, grad_ref, rows_ref, weight_ref, col_moment_ref, new_weight_ref, new_rows_ref, new_cols_ref):
    new_rows_ref[...] = rows_ref[...]
    small = jnp.sum(small_ref[...], axis=0)
    column_sum, scaled_sum = small[:, :WIDTH], small[:, WIDTH : 2 * WIDTH]
    weight_total = jnp.sum(small[:, 2 * WIDTH : 2 * WIDTH + HALF], axis=1, keepdims=True)
    row_mean = jnp.sum(small[:, 2 * WIDTH + HALF :], axis=1, keepdims=True) / D
    new_cols = 0.9 * col_moment_ref[...] + 0.1 * (column_sum / D)
    new_cols_ref[...] = new_cols
    update_total = row_mean * jnp.sum(scaled_sum / new_cols, axis=1, keepdims=True)
    new_rows = to_column(rows_ref[...])
    update = grad_ref[...] * lax.rsqrt(new_rows * new_cols / row_mean)
    entries = D * WIDTH
    update_rms = jnp.sqrt(update_total / entries)
    weight_rms = jnp.sqrt(weight_total / entries + 1e-06)
    factor = 0.05 * weight_rms / jnp.maximum(jnp.float32(1.0), update_rms)
    new_weight_ref[...] = weight_ref[...] - factor * update


def apply_update(small, grad, new_rows, weight, col_moment):
    return pl.pallas_call(
        update_kernel,
        in_specs=[HERE] * 5,
        out_specs=(HERE,) * 3,
        out_shape=(
            jax.ShapeDtypeStruct((ROWS, WIDTH), jnp.float32),
            jax.ShapeDtypeStruct((1, ROWS), jnp.float32),
            jax.ShapeDtypeStruct((1, WIDTH), jnp.float32),
        ),
    )(*(in_vmem(array) for array in (small, grad, new_rows, weight, col_moment)))


def copies_of(value, axes, count):
    return lax.all_to_all(jnp.broadcast_to(value[None], (count,) + value.shape), axes, 0, 0, tiled=True)


def body(inputs, out_grad, weight, row_moment, col_moment):
    parts = token_product(inputs, out_grad)
    parts = lax.all_to_all(parts, AXES, 0, 0, tiled=True, axis_index_groups=near_groups())
    parts = jnp.sum(parts, axis=0).reshape(8, 2, ROWS, WIDTH)
    parts = lax.all_to_all(parts, AXES, 0, 0, tiled=True, axis_index_groups=far_groups())
    mine = pack(parts, weight, row_moment.reshape(1, ROWS))
    other = lax.ppermute(mine, "yh", [(0, 1), (1, 0)])
    grad, row_values, small = statistics(mine, other)
    small = jnp.sum(copies_of(small, ("c", "z"), 16), axis=0)
    small = copies_of(small, ("x", "yl"), 16)
    new_weight, new_rows, new_cols = apply_update(small, grad, row_values, weight, col_moment.reshape(1, WIDTH))
    return (new_weight, new_rows.reshape(ROWS), new_cols.reshape(WIDTH))


def solution(mesh):
    fine = Mesh(mesh.devices.reshape(SIZES), AXES)
    placed = (P(DP, MP), P(DP, None), P(MP + DP, None), P(MP + DP), P())
    return jax.shard_map(
        body,
        mesh=fine,
        in_specs=placed,
        out_specs=(P(MP + DP, None), P(MP + DP), P()),
        check_vma=False,
    )
```
